32 devices in a mesh: group: 2 (over y), seq: 8 (over z, x), chan: 2 (over core).
Axes of the slice: x: 2, y: 2, z: 4, core: 2. Of those that a mesh axis runs over, the one named last changes fastest.
Arguments:
- fresh: bfloat16 [2048, 3, 2048], P(('group', 'seq'), None, 'chan'), parts along dimension 0, may hold values from -6 to 6
- library: bfloat16 [8, 8, 2048], P('seq', None, 'chan'), may hold values from -6 to 6
- block_slot: int32 [8], replicated, may hold values from 0 to 7, each once
- prefix_blocks: int32 [16, 4], P('group'), parts along dimension 0, may hold values from 0 to 7, all different within a row
- short_taps: float32 [3, 3, 2048], P(None, None, 'chan'), may hold values from -4 to 4
- long_filter: float32 [1024, 2048], P('seq', 'chan'), may hold values from -2 to 2
- skip_gain: float32 [2048], P('chan'), may hold values from -6 to 6
Outputs:
- mixed: bfloat16 [2048, 2048], P(('group', 'seq'), 'chan'), parts along dimension 0
The draws below stay inside these ranges and needn't reach their ends.
There are 2 independent parts, one for each index of `group`. The reference program is written for one: setup_inputs(seed, part) draws one part's arguments, and reference() takes and returns one part's arrays. A program takes and returns all parts, laid end to end along the dimension named above; an argument that names none is the same for every part. Nothing has to cross between parts.
Inputs may be any that keep to these rules, and one draw needn't show every extreme that they name: `block_slot`: each number appears once. `prefix_blocks`: every library block is named at least once; the four entries of a row differ.
All inputs are finite; a program needn't handle non-finite values.
Results may differ from the reference program's by a relative error of at most 0.008.
Values may be sent and summed in bfloat16 or wider, within the bound.
A program may use at most 64 MiB of HBM per device.

```python
import math
import jax
import jax.numpy as jnp
from jax import lax

CHANNELS = 2048
TAPS = 3
BLK = 8
TOKENS = 1024
LIB_BLOCKS = 8
PREFIX_BLOCKS = 32


def draw_long_filter(key, part):
    share = 0.5
    chooser = jax.random.uniform(jax.random.fold_in(key, 11), (CHANNELS,), jnp.float32)
    slow_level = jax.random.uniform(jax.random.fold_in(key, 12), (CHANNELS,), jnp.float32, math.log(0.3 / TOKENS), math.log(2.0 / TOKENS))
    fast_level = jax.random.uniform(jax.random.fold_in(key, 13), (CHANNELS,), jnp.float32, math.log(1.0 / 48.0), math.log(1.0 / 24.0))
    rate = jnp.where(chooser < share, jnp.exp(slow_level), jnp.exp(fast_level))
    noise = jax.random.uniform(jax.random.fold_in(key, 14), (TOKENS, CHANNELS), jnp.float32, -1.0, 1.0) * math.sqrt(3.0)
    rough = jax.random.uniform(jax.random.fold_in(key, 15), (TOKENS, CHANNELS), jnp.float32, 0.5, 1.5)
    times = jnp.arange(TOKENS).astype(jnp.float32)[:, None]
    envelope = jnp.sqrt(2.0 * rate)[None, :] * jnp.exp(-rate[None, :] * times)
    values = noise * rough * envelope
    return jnp.clip(values, -2.0, 2.0).astype(jnp.float32)


def steps_of(key, shape, shards, low, high):
    level, own = 1.0, jax.random.fold_in(key, 6)
    for dim, shards_of in shards:
        steps = jnp.exp(jax.random.uniform(jax.random.fold_in(own, dim), (shards_of,), jnp.float32, low / len(shards), high / len(shards)))
        level = level * jnp.repeat(steps, shape[dim] // shards_of).reshape([-1 if axis == dim else 1 for axis in range(len(shape))])
    return level


def different_ones(key, rows, number_of, top, lift):
    order = jax.random.permutation(jax.random.fold_in(key, 1), number_of)
    pull = order
    for power in range(3):
        pull = pull * pull // number_of
    pull = pull * lift // number_of
    tickets = jax.random.randint(jax.random.fold_in(key, 2), (rows, number_of), 0, 4096) + pull
    fixed_rows = jax.random.permutation(jax.random.fold_in(key, 3), rows)[jnp.arange(number_of) % rows]
    tickets = jnp.where(jnp.arange(rows)[:, None] == fixed_rows[None, :], 1 << 14, tickets)
    score = tickets * number_of + jnp.arange(number_of)
    return lax.top_k(score.astype(jnp.int32), top)[1].astype(jnp.int32)


def scatter_about(stream_key, extent, spread, limit, shards=(), dtype=jnp.bfloat16):
    entries = spread * jax.random.normal(stream_key, extent, jnp.float32)
    if shards:
        entries = entries * steps_of(stream_key, extent, shards, -0.22, 0.18)
    return jnp.clip(entries, -limit, limit).astype(dtype)


def setup_inputs(seed: int = 0, part: int = 0) -> dict:
    arg_keys = jax.random.split(jax.random.key(seed), 8)
    own_keys = jax.random.split(jax.random.fold_in(arg_keys[7], part), 8)
    return {
        "fresh": scatter_about(own_keys[0], (TOKENS, 3, CHANNELS), 1.0, 6.0, ((0, 8), (2, 2))),
        "library": scatter_about(arg_keys[1], (LIB_BLOCKS, BLK, CHANNELS), 1.0, 6.0, ((0, 8), (2, 2))),
        "block_slot": jax.random.permutation(arg_keys[2], LIB_BLOCKS).astype(jnp.int32),
        "prefix_blocks": different_ones(own_keys[3], (PREFIX_BLOCKS // 4), LIB_BLOCKS, 4, 8192),
        "short_taps": scatter_about(arg_keys[4], (TAPS, 3, CHANNELS), 0.6, 4.0, ((2, 2),), jnp.float32),
        "long_filter": draw_long_filter(jax.random.fold_in(arg_keys[7], 71), part),
        "skip_gain": scatter_about(arg_keys[6], (CHANNELS,), 1.0, 6.0, ((0, 2),), jnp.float32),
    }


def reference(fresh, library, block_slot, prefix_blocks, short_taps, long_filter, skip_gain):
    slot_ids = block_slot[prefix_blocks.reshape(-1)]
    prefix_len = slot_ids.shape[0] * BLK
    cached = library[slot_ids].reshape(prefix_len, CHANNELS)
    values = jnp.concatenate([cached, fresh[prefix_len:, 2]], axis=0)
    stacked = jnp.stack([fresh[:, 0], fresh[:, 1], values], axis=1).astype(jnp.float32)
    shortened = jnp.zeros(stacked.shape, jnp.float32)
    for offset in range(TAPS):
        shifted = jnp.pad(stacked[:TOKENS - offset], ((offset, 0), (0, 0), (0, 0)))
        shortened = shortened + short_taps[offset][None] * shifted
    gating = shortened[:, 0]
    mixed_in = shortened[:, 1] * shortened[:, 2]
    block_width = math.gcd(CHANNELS, 256)
    block_count = CHANNELS // block_width
    fft_length = 2 * TOKENS

    def convolve(operands):
        signal, impulse = operands
        product = jnp.fft.rfft(signal, n=fft_length, axis=0) * jnp.fft.rfft(impulse, n=fft_length, axis=0)
        return jnp.fft.irfft(product, n=fft_length, axis=0)[:TOKENS]

    signals = mixed_in.reshape(TOKENS, block_count, block_width).transpose(1, 0, 2)
    filters = long_filter.reshape(TOKENS, block_count, block_width).transpose(1, 0, 2)
    convolved = lax.map(convolve, (signals, filters))
    convolved = convolved.transpose(1, 0, 2).reshape(TOKENS, CHANNELS)
    output = gating * (convolved + skip_gain[None, :] * mixed_in)
    return output.astype(jnp.bfloat16)
```

```python
import functools
import math

import jax
import jax.numpy as jnp
import numpy as np
from jax import lax
from jax.experimental import pallas as pl
from jax.experimental.pallas import tpu as pltpu
from jax.sharding import PartitionSpec as P

TAPS = 3
BLK = 8


def from_behind(shard, axis, by):
    count = lax.axis_size(axis)
    pairs = [(i, i + by) for i in range(count) if 0 <= i + by < count]
    return lax.ppermute(shard, axis, pairs)


def exact_dot(pattern, matrix, tensor):
    return jnp.einsum(pattern, matrix, tensor, precision=lax.Precision.HIGHEST)


def turn_angles(numbers, period):
    return (numbers % period).astype(jnp.float32) * (2.0 * math.pi / period)


def long_body(fresh, library, block_slot, prefix_blocks, short_taps, long_filter, skip_gain):
    row_count = fresh.shape[0]
    channels = fresh.shape[2]
    devices = lax.axis_size("seq")
    seq_index = lax.axis_index("seq")
    group_rows = row_count // devices
    period = 2 * row_count * devices
    block_ids = jnp.arange(devices, dtype=jnp.int32)
    mode_ids = jnp.arange(2 * devices, dtype=jnp.int32)
    coarse = turn_angles(mode_ids[:, None] * block_ids[None, :], 2 * devices)
    cos_q = jnp.cos(coarse)
    sin_q = jnp.sin(coarse)
    local_rows = seq_index * group_rows + jnp.arange(group_rows, dtype=jnp.int32)
    twist = turn_angles(mode_ids[:, None] * local_rows[None, :], period)
    twist_cos = jnp.cos(twist)[:, :, None]
    twist_sin = jnp.sin(twist)[:, :, None]
    row_ids = jnp.arange(row_count, dtype=jnp.int32)
    fine_angles = turn_angles(row_ids[:, None] * row_ids[None, :], row_count)
    cos_m = jnp.cos(fine_angles)
    sin_m = jnp.sin(fine_angles)
    first_modes = 2 * seq_index + jnp.arange(2, dtype=jnp.int32)
    back_twist = turn_angles(first_modes[:, None] * row_ids[None, :], period)
    back_cos = jnp.cos(back_twist)[:, :, None]
    back_sin = jnp.sin(back_twist)[:, :, None]

    def to_modes(column):
        real_part = exact_dot("kq,qgc->kgc", cos_q, column)
        imag_part = -exact_dot("kq,qgc->kgc", sin_q, column)
        return jnp.stack(
            [
                real_part * twist_cos + imag_part * twist_sin,
                imag_part * twist_cos - real_part * twist_sin,
            ]
        )

    def to_spectrum(spread):
        real_part = exact_dot("ki,jic->jkc", cos_m, spread[0]) + exact_dot(
            "ki,jic->jkc", sin_m, spread[1]
        )
        imag_part = exact_dot("ki,jic->jkc", cos_m, spread[1]) - exact_dot(
            "ki,jic->jkc", sin_m, spread[0]
        )
        return (real_part, imag_part)

    blocks_here = row_count // BLK
    flat_ids = prefix_blocks.reshape(-1)
    first_block = jnp.minimum(seq_index * blocks_here, flat_ids.shape[0] - blocks_here)
    own_ids = lax.dynamic_slice_in_dim(flat_ids, first_block, blocks_here)
    matches = own_ids[:, None] == jnp.arange(block_slot.shape[0], dtype=jnp.int32)[None, :]
    wanted = jnp.sum(jnp.where(matches, block_slot[None, :], 0), axis=1)
    shards = lax.all_gather(library, "seq", axis=0, tiled=True)
    picker = (wanted[:, None] == jnp.arange(shards.shape[0], dtype=jnp.int32)[None, :]).astype(
        jnp.bfloat16
    )
    gathered = jnp.einsum("bn,nlc->blc", picker, shards, preferred_element_type=jnp.float32)
    cached = gathered.reshape(row_count, channels).astype(jnp.bfloat16)
    values = jnp.where(seq_index < devices // 4, cached, fresh[:, 2])
    stacked = jnp.concatenate([fresh[:, :2], values[:, None]], axis=1)
    previous = from_behind(stacked[row_count - (TAPS - 1) :], "seq", 1)
    extended = jnp.concatenate([previous, stacked], axis=0)
    shortened = jnp.zeros((row_count, 3, channels), jnp.float32)
    for offset in range(TAPS):
        window_start = TAPS - 1 - offset
        shortened = shortened + short_taps[offset][None] * extended[
            window_start : window_start + row_count
        ].astype(jnp.float32)
    gating = shortened[:, 0]
    signal = shortened[:, 1] * shortened[:, 2]
    spread_signal = to_modes(
        lax.all_to_all(signal[None], "seq", split_axis=1, concat_axis=0, tiled=True)
    )
    spread_taps = to_modes(
        lax.all_to_all(long_filter[None], "seq", split_axis=1, concat_axis=0, tiled=True)
    )
    moved_signal, moved_taps = (
        lax.all_to_all(
            spread_signal.astype(jnp.bfloat16), "seq", split_axis=1, concat_axis=2, tiled=True
        ).astype(spread_signal.dtype),
        lax.all_to_all(
            spread_taps.astype(jnp.bfloat16), "seq", split_axis=1, concat_axis=2, tiled=True
        ).astype(spread_taps.dtype),
    )
    sig_real, sig_imag = to_spectrum(moved_signal)
    tap_real, tap_imag = to_spectrum(moved_taps)
    prod_real = sig_real * tap_real - sig_imag * tap_imag
    prod_imag = sig_real * tap_imag + sig_imag * tap_real
    back_real = exact_dot("ki,jic->jkc", cos_m, prod_real) - exact_dot(
        "ki,jic->jkc", sin_m, prod_imag
    )
    back_imag = exact_dot("ki,jic->jkc", cos_m, prod_imag) + exact_dot(
        "ki,jic->jkc", sin_m, prod_real
    )
    turned = jnp.stack(
        [back_real * back_cos - back_imag * back_sin, back_imag * back_cos + back_real * back_sin]
    )
    spread = lax.all_to_all(turned, "seq", split_axis=2, concat_axis=1, tiled=True)
    positions = (
        exact_dot("kq,kgc->qgc", cos_q, spread[0]) - exact_dot("kq,kgc->qgc", sin_q, spread[1])
    ) / period
    convolved = lax.all_to_all(positions, "seq", split_axis=0, concat_axis=1, tiled=True)[0]
    output = gating * (convolved + skip_gain[None, :] * signal)
    return output.astype(jnp.bfloat16)


LANES = 128
FILTER, SIGNAL, BACK, SHELF = 0, 1, 2, 3


def wave_tables(tokens):
    steps = (2 * np.arange(tokens)[:, None] + 1) * np.arange(tokens)[None, :] % (4 * tokens)
    angles = steps.astype(np.float64) * (math.pi / (2 * tokens))
    table = np.concatenate([np.cos(angles), np.sin(angles)], axis=0)
    bf16 = jnp.bfloat16
    high = table.astype(np.float32).astype(bf16)
    low = (table - high.astype(np.float64)).astype(np.float32).astype(bf16)
    return high, low, np.ascontiguousarray(high.T)


def fused_kernel(
    n, pdev, x_ref, lib_ref, slot_ref, pref_ref, taps_ref, filt_ref, skip_ref, fhi_hbm, flo_hbm, g_hbm,
    out_ref,
    fhi, flo, gmat, hsend, hrecv, ssend, srecv, ysend, yrecv, libsend, libg, lastsend, lastg,
    halosend, halorecv, ext, gate, cach, hspec, prod,
    load_sem, send_sem, recv_sem, halo_send, halo_recv, last_send, last_recv,
):
    f32, bf16 = jnp.float32, jnp.bfloat16
    rows = x_ref.shape[1]
    tokens = rows * n
    prefix = pdev * rows
    me = lax.axis_index("seq")
    loads = [
        pltpu.make_async_copy(src, dst, load_sem.at[i])
        for i, (src, dst) in enumerate([(fhi_hbm, fhi), (flo_hbm, flo), (g_hbm, gmat)])
    ]
    for load in loads:
        load.start()

    barrier = pltpu.get_barrier_semaphore()
    for d in range(1, n):
        pl.semaphore_signal(
            barrier, inc=1, device_id={"seq": lax.rem(me + d, n)}, device_id_type=pl.DeviceIdType.MESH
        )

    def remote(src, dst, send, recv, peer):
        return pltpu.make_async_remote_copy(
            src_ref=src, dst_ref=dst, send_sem=send, recv_sem=recv,
            device_id={"seq": peer}, device_id_type=pl.DeviceIdType.MESH,
        )

    def at_rows(ref, index):
        return ref.at[pl.ds(pl.multiple_of(index * rows, rows), rows)]

    def move(kind, d):
        peer = lax.rem(me + d, n)
        source, target = {
            FILTER: (hsend.at[peer], at_rows(hrecv, me)),
            SIGNAL: (ssend.at[peer], at_rows(srecv, me)),
            BACK: (ysend.at[peer], yrecv.at[me]),
            SHELF: (libsend.at[peer], libg.at[me]),
        }[kind]
        return remote(source, target, send_sem.at[kind, d], recv_sem.at[kind, d], peer)

    def arrived(kind):
        for d in range(1, n):
            move(kind, d).wait_recv()

    halo_copy = remote(halosend, halorecv, halo_send, halo_recv, lax.rem(me + 1, n))
    others = [s for s in range(n) if s != pdev]
    last_copy = {
        s: remote(lastsend, lastg.at[me], last_send, last_recv.at[s], pdev) for s in others
    }

    for j in range(3):
        halosend[2 * j : 2 * j + 2] = x_ref[j, rows - 16 :].astype(f32)[14:]
    halosend[6:] = jnp.zeros((2, halosend.shape[1]), f32)
    shelf = lib_ref[0].astype(f32)
    for j in range(n):
        cols = slice(j * LANES, (j + 1) * LANES)
        libsend[j] = shelf[:, cols]
        lastsend[2 * j : 2 * j + 2] = shelf[6:, cols]
        hsend[j] = filt_ref[:, cols].astype(bf16)
    libg[me] = libsend[me]
    lastg[me] = lastsend[...]

    pl.semaphore_wait(barrier, n - 1)

    @pl.when(me < n - 1)
    def _():
        halo_copy.start()

    for s in others:
        @pl.when(me == s)
        def _():
            last_copy[s].start()

    for d in range(1, n):
        move(SHELF, d).start()
    for d in range(1, n):
        move(FILTER, d).start()
    at_rows(hrecv, me)[...] = hsend[me]
    for j in range(3):
        ext[j, 8:] = x_ref[j].astype(f32)

    @pl.when(me == 0)
    def _():
        halorecv[...] = jnp.zeros_like(halorecv)

    @pl.when(me > 0)
    def _():
        halo_copy.wait_recv()

    for j in range(3):
        ext[j, 6:8] = halorecv[2 * j : 2 * j + 2]

    per_row = pref_ref.shape[1]

    def wanted(b):
        return slot_ref[pref_ref[b // per_row, b % per_row]]

    blocks = prefix // BLK

    @pl.when(me == pdev)
    def _():
        for s in others:
            last_copy[s].wait_recv()
        ends = lastg[wanted(blocks - 1)]
        for j in range(n):
            ext[2, 6:8, j * LANES : (j + 1) * LANES] = ends[2 * j : 2 * j + 2]

    def short(j, cols):
        return (
            taps_ref[0, j : j + 1, cols] * ext[j, 8:, cols]
            + taps_ref[1, j : j + 1, cols] * ext[j, 7 : 7 + rows, cols]
            + taps_ref[2, j : j + 1, cols] * ext[j, 6 : 6 + rows, cols]
        )

    in_prefix = me < pdev
    for j in range(n):
        cols = slice(j * LANES, (j + 1) * LANES)
        factor = jnp.where(in_prefix, jnp.float32(1.0), short(2, cols))
        ssend[j] = (short(1, cols) * factor).astype(bf16)
    for d in range(1, n):
        move(SIGNAL, d).start()
    at_rows(srecv, me)[...] = ssend[me]
    for j in range(n):
        cols = slice(j * LANES, (j + 1) * LANES)
        gate[:, cols] = short(0, cols)

    own = pl.ds(pl.multiple_of(me * LANES, LANES), LANES)
    arrived(SHELF)
    cach[:8] = jnp.zeros((8, LANES), f32)
    for b in range(blocks):
        cach[8 + BLK * b : 8 + BLK * (b + 1)] = libg[wanted(b)]

    arrived(FILTER)
    for load in loads:
        load.wait()
    tile = 512
    skip = skip_ref[:, own]

    def filter_tile(i, carry):
        span = pl.ds(pl.multiple_of(i * tile, tile), tile)
        spec = jnp.dot(fhi[span], hrecv[...], preferred_element_type=f32)
        spec += jnp.dot(flo[span], hrecv[...], preferred_element_type=f32)
        hspec[span] = spec + jnp.where(i < tokens // tile, skip, 0.0)
        return carry

    lax.fori_loop(0, 2 * tokens // tile, filter_tile, 0)

    arrived(SIGNAL)
    cached = (
        taps_ref[0, 2:3, own] * cach[8:]
        + taps_ref[1, 2:3, own] * cach[7 : 7 + prefix]
        + taps_ref[2, 2:3, own] * cach[6 : 6 + prefix]
    )
    srecv[:prefix] = (srecv[:prefix].astype(f32) * cached).astype(bf16)

    half = 256

    def signal_tile(i, carry):
        upper = pl.ds(pl.multiple_of(i * half, half), half)
        lower = pl.ds(pl.multiple_of(tokens + i * half, half), half)
        even = jnp.dot(fhi[upper], srecv[...], preferred_element_type=f32)
        even += jnp.dot(flo[upper], srecv[...], preferred_element_type=f32)
        odd = jnp.dot(fhi[lower], srecv[...], preferred_element_type=f32)
        odd += jnp.dot(flo[lower], srecv[...], preferred_element_type=f32)
        tap_even, tap_odd = hspec[upper] * (1.0 / tokens), hspec[lower] * (1.0 / tokens)
        for span, value in (
            (upper, even * tap_even - odd * tap_odd),
            (lower, even * tap_odd + odd * tap_even),
        ):
            high = value.astype(bf16)
            prod[span, :LANES] = high
            prod[span, LANES:] = (value - high.astype(f32)).astype(bf16)
        return carry

    lax.fori_loop(0, tokens // half, signal_tile, 0)

    pair = 2 * rows

    def back_tile(i, carry):
        span = pl.ds(pl.multiple_of(i * pair, pair), pair)
        both = jnp.dot(gmat[span], prod[...], preferred_element_type=f32)
        value = (both[:, :LANES] + both[:, LANES:]).astype(bf16)
        ysend[2 * i] = value[:rows]
        ysend[2 * i + 1] = value[rows:]
        return carry

    lax.fori_loop(0, n // 2, back_tile, 0)
    for d in range(1, n):
        move(BACK, d).start()
    yrecv[me] = ysend[me]
    arrived(BACK)
    for j in range(n):
        cols = slice(j * LANES, (j + 1) * LANES)
        out_ref[:, cols] = (gate[:, cols] * yrecv[j].astype(f32)).astype(bf16)

    @pl.when(me < n - 1)
    def _():
        halo_copy.wait_send()

    @pl.when(me != pdev)
    def _():
        last_copy[others[0]].wait_send()

    for kind in (SHELF, FILTER, SIGNAL, BACK):
        for d in range(1, n):
            move(kind, d).wait_send()


def fused_body(n, fresh, library, block_slot, prefix_blocks, short_taps, long_filter, skip_gain):
    rows, channels = fresh.shape[0], fresh.shape[2]
    tokens = rows * n
    prefix = prefix_blocks.size * BLK
    f32, bf16 = jnp.float32, jnp.bfloat16
    high, low, turned = wave_tables(tokens)
    vmem = pl.BlockSpec(memory_space=pltpu.VMEM)
    smem = pl.BlockSpec(memory_space=pltpu.SMEM)
    far = pl.BlockSpec(memory_space=pl.ANY)
    dma = pltpu.SemaphoreType.DMA
    return pl.pallas_call(
        functools.partial(fused_kernel, n, prefix // rows),
        out_shape=jax.ShapeDtypeStruct((rows, channels), bf16),
        in_specs=[vmem, vmem, smem, smem, vmem, vmem, vmem, far, far, far],
        out_specs=vmem,
        scratch_shapes=[
            pltpu.VMEM((2 * tokens, tokens), bf16),
            pltpu.VMEM((2 * tokens, tokens), bf16),
            pltpu.VMEM((tokens, 2 * tokens), bf16),
            pltpu.VMEM((n, rows, LANES), bf16),
            pltpu.VMEM((tokens, LANES), bf16),
            pltpu.VMEM((n, rows, LANES), bf16),
            pltpu.VMEM((tokens, LANES), bf16),
            pltpu.VMEM((n, rows, LANES), bf16),
            pltpu.VMEM((n, rows, LANES), bf16),
            pltpu.VMEM((n, BLK, LANES), f32),
            pltpu.VMEM((n, BLK, LANES), f32),
            pltpu.VMEM((2 * n, LANES), f32),
            pltpu.VMEM((n, 2 * n, LANES), f32),
            pltpu.VMEM((8, channels), f32),
            pltpu.VMEM((8, channels), f32),
            pltpu.VMEM((3, rows + 8, channels), f32),
            pltpu.VMEM((rows, channels), f32),
            pltpu.VMEM((prefix + 8, LANES), f32),
            pltpu.VMEM((2 * tokens, LANES), f32),
            pltpu.VMEM((2 * tokens, 2 * LANES), bf16),
            dma((3,)),
            dma((4, n)),
            dma((4, n)),
            dma(()),
            dma(()),
            dma(()),
            dma((n,)),
        ],
        compiler_params=pltpu.CompilerParams(
            collective_id=0, has_side_effects=True, vmem_limit_bytes=50 * 1024 * 1024
        ),
    )(
        jnp.transpose(fresh, (1, 0, 2)), library, block_slot, prefix_blocks, short_taps, long_filter,
        skip_gain[None, :], jnp.asarray(high), jnp.asarray(low), jnp.asarray(turned),
    )


def body(n, fresh, library, block_slot, prefix_blocks, short_taps, long_filter, skip_gain):
    rows, channels = fresh.shape[0], fresh.shape[2]
    prefix = prefix_blocks.size * BLK
    small = (
        rows * n <= 1024
        and rows % 128 == 0
        and channels == n * LANES
        and library.shape[0] == 1
        and prefix % rows == 0
        and 0 < prefix // rows < n
    )
    chosen = functools.partial(fused_body, n) if small else long_body
    return chosen(fresh, library, block_slot, prefix_blocks, short_taps, long_filter, skip_gain)


def solution(mesh):
    return jax.shard_map(
        functools.partial(body, mesh.shape["seq"]),
        mesh=mesh,
        in_specs=(
            P(("group", "seq"), None, "chan"),
            P("seq", None, "chan"),
            P(),
            P("group", None),
            P(None, None, "chan"),
            P("seq", "chan"),
            P("chan"),
        ),
        out_specs=P(("group", "seq"), "chan"),
        check_vma=False,
    )
```

```python
import functools
import math

import jax
import jax.numpy as jnp
import numpy as np
from jax import lax
from jax.experimental import pallas as pl
from jax.experimental.pallas import tpu as pltpu
from jax.sharding import PartitionSpec as P

TAPS = 3
BLK = 8


def from_behind(shard, axis, by):
    count = lax.axis_size(axis)
    pairs = [(i, i + by) for i in range(count) if 0 <= i + by < count]
    return lax.ppermute(shard, axis, pairs)


def exact_dot(pattern, matrix, tensor):
    return jnp.einsum(pattern, matrix, tensor, precision=lax.Precision.HIGHEST)


def turn_angles(numbers, period):
    return (numbers % period).astype(jnp.float32) * (2.0 * math.pi / period)


def long_body(fresh, library, block_slot, prefix_blocks, short_taps, long_filter, skip_gain):
    row_count = fresh.shape[0]
    channels = fresh.shape[2]
    devices = lax.axis_size("seq")
    seq_index = lax.axis_index("seq")
    group_rows = row_count // devices
    period = 2 * row_count * devices
    block_ids = jnp.arange(devices, dtype=jnp.int32)
    mode_ids = jnp.arange(2 * devices, dtype=jnp.int32)
    coarse = turn_angles(mode_ids[:, None] * block_ids[None, :], 2 * devices)
    cos_q = jnp.cos(coarse)
    sin_q = jnp.sin(coarse)
    local_rows = seq_index * group_rows + jnp.arange(group_rows, dtype=jnp.int32)
    twist = turn_angles(mode_ids[:, None] * local_rows[None, :], period)
    twist_cos = jnp.cos(twist)[:, :, None]
    twist_sin = jnp.sin(twist)[:, :, None]
    row_ids = jnp.arange(row_count, dtype=jnp.int32)
    fine_angles = turn_angles(row_ids[:, None] * row_ids[None, :], row_count)
    cos_m = jnp.cos(fine_angles)
    sin_m = jnp.sin(fine_angles)
    first_modes = 2 * seq_index + jnp.arange(2, dtype=jnp.int32)
    back_twist = turn_angles(first_modes[:, None] * row_ids[None, :], period)
    back_cos = jnp.cos(back_twist)[:, :, None]
    back_sin = jnp.sin(back_twist)[:, :, None]

    def to_modes(column):
        real_part = exact_dot("kq,qgc->kgc", cos_q, column)
        imag_part = -exact_dot("kq,qgc->kgc", sin_q, column)
        return jnp.stack(
            [
                real_part * twist_cos + imag_part * twist_sin,
                imag_part * twist_cos - real_part * twist_sin,
            ]
        )

    def to_spectrum(spread):
        real_part = exact_dot("ki,jic->jkc", cos_m, spread[0]) + exact_dot(
            "ki,jic->jkc", sin_m, spread[1]
        )
        imag_part = exact_dot("ki,jic->jkc", cos_m, spread[1]) - exact_dot(
            "ki,jic->jkc", sin_m, spread[0]
        )
        return (real_part, imag_part)

    blocks_here = row_count // BLK
    flat_ids = prefix_blocks.reshape(-1)
    first_block = jnp.minimum(seq_index * blocks_here, flat_ids.shape[0] - blocks_here)
    own_ids = lax.dynamic_slice_in_dim(flat_ids, first_block, blocks_here)
    matches = own_ids[:, None] == jnp.arange(block_slot.shape[0], dtype=jnp.int32)[None, :]
    wanted = jnp.sum(jnp.where(matches, block_slot[None, :], 0), axis=1)
    shards = lax.all_gather(library, "seq", axis=0, tiled=True)
    picker = (wanted[:, None] == jnp.arange(shards.shape[0], dtype=jnp.int32)[None, :]).astype(
        jnp.bfloat16
    )
    gathered = jnp.einsum("bn,nlc->blc", picker, shards, preferred_element_type=jnp.float32)
    cached = gathered.reshape(row_count, channels).astype(jnp.bfloat16)
    values = jnp.where(seq_index < devices // 4, cached, fresh[:, 2])
    stacked = jnp.concatenate([fresh[:, :2], values[:, None]], axis=1)
    previous = from_behind(stacked[row_count - (TAPS - 1) :], "seq", 1)
    extended = jnp.concatenate([previous, stacked], axis=0)
    shortened = jnp.zeros((row_count, 3, channels), jnp.float32)
    for offset in range(TAPS):
        window_start = TAPS - 1 - offset
        shortened = shortened + short_taps[offset][None] * extended[
            window_start : window_start + row_count
        ].astype(jnp.float32)
    gating = shortened[:, 0]
    signal = shortened[:, 1] * shortened[:, 2]
    spread_signal = to_modes(
        lax.all_to_all(signal[None], "seq", split_axis=1, concat_axis=0, tiled=True)
    )
    spread_taps = to_modes(
        lax.all_to_all(long_filter[None], "seq", split_axis=1, concat_axis=0, tiled=True)
    )
    moved_signal, moved_taps = (
        lax.all_to_all(
            spread_signal.astype(jnp.bfloat16), "seq", split_axis=1, concat_axis=2, tiled=True
        ).astype(spread_signal.dtype),
        lax.all_to_all(
            spread_taps.astype(jnp.bfloat16), "seq", split_axis=1, concat_axis=2, tiled=True
        ).astype(spread_taps.dtype),
    )
    sig_real, sig_imag = to_spectrum(moved_signal)
    tap_real, tap_imag = to_spectrum(moved_taps)
    prod_real = sig_real * tap_real - sig_imag * tap_imag
    prod_imag = sig_real * tap_imag + sig_imag * tap_real
    back_real = exact_dot("ki,jic->jkc", cos_m, prod_real) - exact_dot(
        "ki,jic->jkc", sin_m, prod_imag
    )
    back_imag = exact_dot("ki,jic->jkc", cos_m, prod_imag) + exact_dot(
        "ki,jic->jkc", sin_m, prod_real
    )
    turned = jnp.stack(
        [back_real * back_cos - back_imag * back_sin, back_imag * back_cos + back_real * back_sin]
    )
    spread = lax.all_to_all(turned, "seq", split_axis=2, concat_axis=1, tiled=True)
    positions = (
        exact_dot("kq,kgc->qgc", cos_q, spread[0]) - exact_dot("kq,kgc->qgc", sin_q, spread[1])
    ) / period
    convolved = lax.all_to_all(positions, "seq", split_axis=0, concat_axis=1, tiled=True)[0]
    output = gating * (convolved + skip_gain[None, :] * signal)
    return output.astype(jnp.bfloat16)


LANES = 128
FILTER, SIGNAL, BACK, SHELF, ACROSS = range(5)


def wave_tables(tokens):
    steps = (2 * np.arange(tokens)[:, None] + 1) * np.arange(tokens)[None, :] % (4 * tokens)
    angles = steps.astype(np.float64) * (math.pi / (2 * tokens))
    table = np.concatenate([np.cos(angles), np.sin(angles)], axis=0)
    bf16 = jnp.bfloat16
    high = table.astype(np.float32).astype(bf16)
    low = (table - high.astype(np.float64)).astype(np.float32).astype(bf16)
    return high, low, np.ascontiguousarray(high.T)


def fused_kernel(
    n, pdev, x_hbm, lib_hbm, slot_hbm, pref_hbm, taps_hbm, filt_hbm, skip_hbm, fhi_hbm, flo_hbm, g_hbm,
    out_ref,
    x_ref, lib_ref, slot_ref, pref_ref, taps_ref, filt_ref, skip_ref, fhi, flo, gmat, hsend, hrecv, ssend, srecv, ysend, yrecv, libsend, libg, lastsend, lastg,
    halosend, halorecv, ext, gate, cach, hspec, prod, rising,
    load_sem, send_sem, recv_sem, halo_send, halo_recv, last_send, last_recv,
):
    f32, bf16 = jnp.float32, jnp.bfloat16
    rows = x_ref.shape[1]
    tokens = rows * n
    prefix = pdev * rows
    duo = rows // 2
    steps = tokens // 2
    phases = range(2)
    wide = [slice(p * LANES, (p + 1) * LANES) for p in phases]
    me = lax.axis_index("seq")
    group = lax.axis_index("group")
    share = rows // 4
    barrier = pltpu.get_barrier_semaphore()
    for d in range(1, n):
        pl.semaphore_signal(
            barrier, inc=1, device_id={"seq": lax.rem(me + d, n)}, device_id_type=pl.DeviceIdType.MESH
        )
    pl.semaphore_signal(
        barrier, inc=1, device_id={"group": 1 - group}, device_id_type=pl.DeviceIdType.MESH
    )
    operands = [
        *((filt_hbm.at[:, j * LANES : (j + 1) * LANES], filt_ref.at[j]) for j in range(n)), (x_hbm, x_ref), (lib_hbm, lib_ref), (taps_hbm, taps_ref),
        (slot_hbm, slot_ref), (pref_hbm, pref_ref), (skip_hbm, skip_ref),
        (fhi_hbm, fhi), (flo_hbm, flo), (g_hbm, gmat),
    ]
    loads = [pltpu.make_async_copy(src, dst, load_sem.at[i]) for i, (src, dst) in enumerate(operands)]
    for load in loads:
        load.start()
    load_filter, load_x, load_small, load_tables = loads[:n], loads[n], loads[n + 1 : -3], loads[-3:]

    half_ring = n // 2
    order = [half_ring] + [d for k in range(1, half_ring) for d in (half_ring + k, half_ring - k)]

    def lanes_of(index):
        if isinstance(index, int):
            return pl.ds(index * LANES, LANES)
        return pl.ds(pl.multiple_of(index * LANES, LANES), LANES)

    def remote(src, dst, send, recv, peer):
        return pltpu.make_async_remote_copy(
            src_ref=src, dst_ref=dst, send_sem=send, recv_sem=recv,
            device_id={"seq": peer}, device_id_type=pl.DeviceIdType.MESH,
        )

    def at_rows(ref, index):
        return ref.at[pl.ds(pl.multiple_of(index * duo, duo), duo)]

    def at_share(ref, index):
        return ref.at[pl.ds(pl.multiple_of(index * duo + group * share, share), share)]

    def across(d):
        part = at_share(hrecv, lax.rem(me + n - d, n))
        return pltpu.make_async_remote_copy(
            src_ref=part, dst_ref=part, send_sem=send_sem.at[ACROSS, d], recv_sem=recv_sem.at[ACROSS, d],
            device_id={"group": 1 - group}, device_id_type=pl.DeviceIdType.MESH,
        )

    def move(kind, d):
        peer = lax.rem(me + d, n)
        source, target = {
            FILTER: (
                hsend.at[peer, pl.ds(pl.multiple_of(group * share, share), share)],
                at_share(hrecv, me),
            ),
            SIGNAL: (ssend.at[peer], at_rows(srecv, me)),
            BACK: (ysend.at[peer], yrecv.at[me]),
            SHELF: (libsend.at[peer], libg.at[me]),
        }[kind]
        return remote(source, target, send_sem.at[kind, d], recv_sem.at[kind, d], peer)

    def arrived(kind):
        for d in range(1, n):
            move(kind, d).wait_recv()

    halo_copy = remote(halosend, halorecv, halo_send, halo_recv, lax.rem(me + 1, n))
    others = [s for s in range(n) if s != pdev]
    last_copy = {
        s: remote(lastsend, lastg.at[me], last_send, last_recv.at[s], pdev) for s in others
    }

    def strided(start, count):
        return pl.ds(start, count, stride=2)

    for j in range(n):
        load_filter[j].wait()
        for p in phases:
            hsend[j, :, wide[p]] = filt_ref[j, strided(p, duo), :].astype(bf16)
    at_rows(hrecv, me)[...] = hsend[me]
    load_x.wait()
    for j in range(3):
        for c in range(n):
            ext[j, c, 8:] = x_ref[j, :, c * LANES : (c + 1) * LANES].astype(f32)
        halosend[2 * j : 2 * j + 2] = x_ref[j, rows - 16 :].astype(f32)[14:]
    halosend[6:] = jnp.zeros((2, halosend.shape[1]), f32)
    for load in load_small:
        load.wait()
    shelf = lib_ref[0].astype(f32)
    for j in range(n):
        cols = slice(j * LANES, (j + 1) * LANES)
        libsend[j] = shelf[:, cols]
        lastsend[2 * j : 2 * j + 2] = shelf[6:, cols]
    libg[me] = libsend[me]
    lastg[me] = lastsend[...]

    pl.semaphore_wait(barrier, n)

    @pl.when(me < n - 1)
    def _():
        halo_copy.start()

    for s in others:
        @pl.when(me == s)
        def _():
            last_copy[s].start()

    for d in order:
        move(FILTER, d).start()
    for d in order:
        move(SHELF, d).start()
    @pl.when(me == 0)
    def _():
        halorecv[...] = jnp.zeros_like(halorecv)

    @pl.when(me > 0)
    def _():
        halo_copy.wait_recv()

    for j in range(3):
        for c in range(n):
            ext[j, c, 6:8] = halorecv[2 * j : 2 * j + 2, c * LANES : (c + 1) * LANES]

    per_row = pref_ref.shape[0]

    def wanted(b):
        return slot_ref[pref_ref[b % per_row, b // per_row]]

    blocks = prefix // BLK

    @pl.when(me == pdev)
    def _():
        for s in others:
            last_copy[s].wait_recv()
        ends = lastg[wanted(blocks - 1)]
        for j in range(n):
            ext[2, j, 6:8] = ends[2 * j : 2 * j + 2]

    def short(j, p, index):
        cols = lanes_of(index)
        return (
            taps_ref[0, j : j + 1, cols] * ext[j, index, strided(8 + p, duo), :]
            + taps_ref[1, j : j + 1, cols] * ext[j, index, strided(7 + p, duo), :]
            + taps_ref[2, j : j + 1, cols] * ext[j, index, strided(6 + p, duo), :]
        )

    in_prefix = me < pdev

    def pack_signal(index):
        for p in phases:
            factor = jnp.where(in_prefix, jnp.float32(1.0), short(2, p, index))
            ssend[index, :, wide[p]] = (short(1, p, index) * factor).astype(bf16)

    for d in order:
        pack_signal(lax.rem(me + d, n))
        move(SIGNAL, d).start()
    pack_signal(me)
    at_rows(srecv, me)[...] = ssend[me]
    for d in range(1, n):
        move(FILTER, d).wait_recv()
        across(d).start()

    own = lanes_of(me)
    arrived(SHELF)
    cach[:8] = jnp.zeros((8, LANES), f32)
    for b in range(blocks):
        cach[8 + BLK * b : 8 + BLK * (b + 1)] = libg[wanted(b)]

    for d in range(1, n):
        across(d).wait_recv()
    for load in load_tables:
        load.wait()
    tile = 256
    skip = skip_ref[own].reshape(1, LANES)

    def filter_tile(i, carry):
        span = pl.ds(pl.multiple_of(i * tile, tile), tile)
        spec = jnp.dot(fhi[span], hrecv[...], preferred_element_type=f32)
        spec += jnp.dot(flo[span], hrecv[...], preferred_element_type=f32)
        hspec[span, wide[0]] = spec[:, wide[0]] + jnp.where(i < steps // tile, skip, 0.0)
        hspec[span, wide[1]] = spec[:, wide[1]]
        return carry

    lax.fori_loop(0, 2 * steps // tile, filter_tile, 0)

    for j in range(n):
        for p in phases:
            gate[j, :, wide[p]] = short(0, p, j)

    early = prefix // 2
    cached = [
        taps_ref[0, 2:3, own] * cach[strided(8 + p, early), :]
        + taps_ref[1, 2:3, own] * cach[strided(7 + p, early), :]
        + taps_ref[2, 2:3, own] * cach[strided(6 + p, early), :]
        for p in phases
    ]
    arrived(SIGNAL)
    for p in phases:
        srecv[:early, wide[p]] = (srecv[:early, wide[p]].astype(f32) * cached[p]).astype(bf16)

    half = 128

    def times(first, second):
        return (
            first[0] * second[0] - first[1] * second[1],
            first[0] * second[1] + first[1] * second[0],
        )

    def signal_tile(i, carry):
        spans = [pl.ds(pl.multiple_of(part * steps + i * half, half), half) for part in range(2)]
        waves = [
            jnp.dot(fhi[span], srecv[...], preferred_element_type=f32)
            + jnp.dot(flo[span], srecv[...], preferred_element_type=f32)
            for span in spans
        ]
        taps = [hspec[span] * (1.0 / steps) for span in spans]
        turn = [fhi[span, 1:2].astype(f32) + flo[span, 1:2].astype(f32) for span in spans]
        even, odd = ([wave[:, wide[p]] for wave in waves] for p in phases)
        tap_even, tap_odd = ([tap[:, wide[p]] for tap in taps] for p in phases)
        late = times(times(odd, tap_odd), turn)
        even_even, even_odd, odd_even = times(even, tap_even), times(even, tap_odd), times(odd, tap_even)
        for part in range(2):
            for p, value in ((0, even_even[part] + late[part]), (1, even_odd[part] + odd_even[part])):
                high = value.astype(bf16)
                prod[spans[part], wide[p]] = high
                prod[spans[part], (2 + p) * LANES : (3 + p) * LANES] = (
                    value - high.astype(f32)
                ).astype(bf16)
        return carry

    lax.fori_loop(0, steps // half, signal_tile, 0)

    reach = half_ring * duo
    for k in (1, 0):
        side = lax.rem(me // half_ring + k, 2)
        span = pl.ds(pl.multiple_of(side * reach, reach), reach)
        both = jnp.dot(gmat[span], prod[...], preferred_element_type=f32)
        value = (both[:, : 2 * LANES] + both[:, 2 * LANES :]).astype(bf16)
        for r in range(half_ring):
            target = side * half_ring + r
            ysend[target] = value[r * duo : (r + 1) * duo]

            @pl.when(target != me)
            def _():
                move(BACK, lax.rem(target - me + n, n)).start()

    def finish(source, value):
        cols = lanes_of(source)
        for p in phases:
            rising[strided(p, duo), :] = gate[source, :, wide[p]] * value[:, wide[p]].astype(f32)
        out_ref[:, cols] = rising[...].astype(bf16)

    finish(me, ysend[me])
    for d in range(1, n):
        move(BACK, d).wait_recv()
        source = lax.rem(me + n - d, n)
        finish(source, yrecv[source])

    @pl.when(me < n - 1)
    def _():
        halo_copy.wait_send()

    @pl.when(me != pdev)
    def _():
        last_copy[others[0]].wait_send()

    for kind in (SHELF, FILTER, SIGNAL, BACK):
        for d in range(1, n):
            move(kind, d).wait_send()
    for d in range(1, n):
        across(d).wait_send()


def fused_body(n, fresh, library, block_slot, prefix_blocks, short_taps, long_filter, skip_gain):
    rows, channels = fresh.shape[0], fresh.shape[2]
    tokens = rows * n
    prefix = prefix_blocks.size * BLK
    f32, bf16 = jnp.float32, jnp.bfloat16
    high, low, turned = wave_tables(tokens // 2)
    far = pl.BlockSpec(memory_space=pltpu.HBM)
    dma = pltpu.SemaphoreType.DMA
    return pl.pallas_call(
        functools.partial(fused_kernel, n, prefix // rows),
        out_shape=jax.ShapeDtypeStruct((rows, channels), bf16),
        in_specs=[far] * 10,
        out_specs=pl.BlockSpec(memory_space=pltpu.VMEM),
        scratch_shapes=[
            pltpu.VMEM((3, rows, channels), bf16),
            pltpu.VMEM(library.shape, bf16),
            pltpu.SMEM(block_slot.shape, jnp.int32),
            pltpu.SMEM(prefix_blocks.shape[::-1], jnp.int32),
            pltpu.VMEM(short_taps.shape, f32),
            pltpu.VMEM((n, rows, LANES), f32),
            pltpu.VMEM(skip_gain.shape, f32),
            pltpu.VMEM((tokens, tokens // 2), bf16),
            pltpu.VMEM((tokens, tokens // 2), bf16),
            pltpu.VMEM((tokens // 2, tokens), bf16),
            pltpu.VMEM((n, rows // 2, 2 * LANES), bf16),
            pltpu.VMEM((tokens // 2, 2 * LANES), bf16),
            pltpu.VMEM((n, rows // 2, 2 * LANES), bf16),
            pltpu.VMEM((tokens // 2, 2 * LANES), bf16),
            pltpu.VMEM((n, rows // 2, 2 * LANES), bf16),
            pltpu.VMEM((n, rows // 2, 2 * LANES), bf16),
            pltpu.VMEM((n, BLK, LANES), f32),
            pltpu.VMEM((n, BLK, LANES), f32),
            pltpu.VMEM((2 * n, LANES), f32),
            pltpu.VMEM((n, 2 * n, LANES), f32),
            pltpu.VMEM((8, channels), f32),
            pltpu.VMEM((8, channels), f32),
            pltpu.VMEM((3, n, rows + 8, LANES), f32),
            pltpu.VMEM((n, rows // 2, 2 * LANES), f32),
            pltpu.VMEM((prefix + 8, LANES), f32),
            pltpu.VMEM((tokens, 2 * LANES), f32),
            pltpu.VMEM((tokens, 4 * LANES), bf16),
            pltpu.VMEM((rows, LANES), f32),
            dma((9 + n,)),
            dma((5, n)),
            dma((5, n)),
            dma(()),
            dma(()),
            dma(()),
            dma((n,)),
        ],
        compiler_params=pltpu.CompilerParams(
            collective_id=0, has_side_effects=True, vmem_limit_bytes=63 * 1024 * 1024
        ),
    )(
        jnp.transpose(fresh, (1, 0, 2)), library, block_slot, prefix_blocks.T, short_taps, long_filter,
        skip_gain, jnp.asarray(high), jnp.asarray(low), jnp.asarray(turned),
    )


def body(groups, n, fresh, library, block_slot, prefix_blocks, short_taps, long_filter, skip_gain):
    rows, channels = fresh.shape[0], fresh.shape[2]
    prefix = prefix_blocks.size * BLK
    small = (
        groups == 2
        and rows * n <= 1024
        and rows % 128 == 0
        and channels == n * LANES
        and library.shape[0] == 1
        and prefix % rows == 0
        and 0 < prefix // rows <= n // 2
        and n % 2 == 0
    )
    chosen = functools.partial(fused_body, n) if small else long_body
    return chosen(fresh, library, block_slot, prefix_blocks, short_taps, long_filter, skip_gain)


def solution(mesh):
    return jax.shard_map(
        functools.partial(body, mesh.shape["group"], mesh.shape["seq"]),
        mesh=mesh,
        in_specs=(
            P(("group", "seq"), None, "chan"),
            P("seq", None, "chan"),
            P(),
            P("group", None),
            P(None, None, "chan"),
            P("seq", "chan"),
            P("chan"),
        ),
        out_specs=P(("group", "seq"), "chan"),
        check_vma=False,
    )
```

```python
import functools
import math

import jax
import jax.numpy as jnp
import numpy as np
from jax import lax
from jax.experimental import pallas as pl
from jax.experimental.pallas import tpu as pltpu
from jax.sharding import PartitionSpec as P

TAPS = 3
BLK = 8


def from_behind(shard, axis, by):
    count = lax.axis_size(axis)
    pairs = [(i, i + by) for i in range(count) if 0 <= i + by < count]
    return lax.ppermute(shard, axis, pairs)


def exact_dot(pattern, matrix, tensor):
    return jnp.einsum(pattern, matrix, tensor, precision=lax.Precision.HIGHEST)


def turn_angles(numbers, period):
    return (numbers % period).astype(jnp.float32) * (2.0 * math.pi / period)


def long_body(fresh, library, block_slot, prefix_blocks, short_taps, long_filter, skip_gain):
    row_count = fresh.shape[0]
    channels = fresh.shape[2]
    devices = lax.axis_size("seq")
    seq_index = lax.axis_index("seq")
    group_rows = row_count // devices
    period = 2 * row_count * devices
    block_ids = jnp.arange(devices, dtype=jnp.int32)
    mode_ids = jnp.arange(2 * devices, dtype=jnp.int32)
    coarse = turn_angles(mode_ids[:, None] * block_ids[None, :], 2 * devices)
    cos_q = jnp.cos(coarse)
    sin_q = jnp.sin(coarse)
    local_rows = seq_index * group_rows + jnp.arange(group_rows, dtype=jnp.int32)
    twist = turn_angles(mode_ids[:, None] * local_rows[None, :], period)
    twist_cos = jnp.cos(twist)[:, :, None]
    twist_sin = jnp.sin(twist)[:, :, None]
    row_ids = jnp.arange(row_count, dtype=jnp.int32)
    fine_angles = turn_angles(row_ids[:, None] * row_ids[None, :], row_count)
    cos_m = jnp.cos(fine_angles)
    sin_m = jnp.sin(fine_angles)
    first_modes = 2 * seq_index + jnp.arange(2, dtype=jnp.int32)
    back_twist = turn_angles(first_modes[:, None] * row_ids[None, :], period)
    back_cos = jnp.cos(back_twist)[:, :, None]
    back_sin = jnp.sin(back_twist)[:, :, None]

    def to_modes(column):
        real_part = exact_dot("kq,qgc->kgc", cos_q, column)
        imag_part = -exact_dot("kq,qgc->kgc", sin_q, column)
        return jnp.stack(
            [
                real_part * twist_cos + imag_part * twist_sin,
                imag_part * twist_cos - real_part * twist_sin,
            ]
        )

    def to_spectrum(spread):
        real_part = exact_dot("ki,jic->jkc", cos_m, spread[0]) + exact_dot(
            "ki,jic->jkc", sin_m, spread[1]
        )
        imag_part = exact_dot("ki,jic->jkc", cos_m, spread[1]) - exact_dot(
            "ki,jic->jkc", sin_m, spread[0]
        )
        return (real_part, imag_part)

    blocks_here = row_count // BLK
    flat_ids = prefix_blocks.reshape(-1)
    first_block = jnp.minimum(seq_index * blocks_here, flat_ids.shape[0] - blocks_here)
    own_ids = lax.dynamic_slice_in_dim(flat_ids, first_block, blocks_here)
    matches = own_ids[:, None] == jnp.arange(block_slot.shape[0], dtype=jnp.int32)[None, :]
    wanted = jnp.sum(jnp.where(matches, block_slot[None, :], 0), axis=1)
    shards = lax.all_gather(library, "seq", axis=0, tiled=True)
    picker = (wanted[:, None] == jnp.arange(shards.shape[0], dtype=jnp.int32)[None, :]).astype(
        jnp.bfloat16
    )
    gathered = jnp.einsum("bn,nlc->blc", picker, shards, preferred_element_type=jnp.float32)
    cached = gathered.reshape(row_count, channels).astype(jnp.bfloat16)
    values = jnp.where(seq_index < devices // 4, cached, fresh[:, 2])
    stacked = jnp.concatenate([fresh[:, :2], values[:, None]], axis=1)
    previous = from_behind(stacked[row_count - (TAPS - 1) :], "seq", 1)
    extended = jnp.concatenate([previous, stacked], axis=0)
    shortened = jnp.zeros((row_count, 3, channels), jnp.float32)
    for offset in range(TAPS):
        window_start = TAPS - 1 - offset
        shortened = shortened + short_taps[offset][None] * extended[
            window_start : window_start + row_count
        ].astype(jnp.float32)
    gating = shortened[:, 0]
    signal = shortened[:, 1] * shortened[:, 2]
    spread_signal = to_modes(
        lax.all_to_all(signal[None], "seq", split_axis=1, concat_axis=0, tiled=True)
    )
    spread_taps = to_modes(
        lax.all_to_all(long_filter[None], "seq", split_axis=1, concat_axis=0, tiled=True)
    )
    moved_signal, moved_taps = (
        lax.all_to_all(
            spread_signal.astype(jnp.bfloat16), "seq", split_axis=1, concat_axis=2, tiled=True
        ).astype(spread_signal.dtype),
        lax.all_to_all(
            spread_taps.astype(jnp.bfloat16), "seq", split_axis=1, concat_axis=2, tiled=True
        ).astype(spread_taps.dtype),
    )
    sig_real, sig_imag = to_spectrum(moved_signal)
    tap_real, tap_imag = to_spectrum(moved_taps)
    prod_real = sig_real * tap_real - sig_imag * tap_imag
    prod_imag = sig_real * tap_imag + sig_imag * tap_real
    back_real = exact_dot("ki,jic->jkc", cos_m, prod_real) - exact_dot(
        "ki,jic->jkc", sin_m, prod_imag
    )
    back_imag = exact_dot("ki,jic->jkc", cos_m, prod_imag) + exact_dot(
        "ki,jic->jkc", sin_m, prod_real
    )
    turned = jnp.stack(
        [back_real * back_cos - back_imag * back_sin, back_imag * back_cos + back_real * back_sin]
    )
    spread = lax.all_to_all(turned, "seq", split_axis=2, concat_axis=1, tiled=True)
    positions = (
        exact_dot("kq,kgc->qgc", cos_q, spread[0]) - exact_dot("kq,kgc->qgc", sin_q, spread[1])
    ) / period
    convolved = lax.all_to_all(positions, "seq", split_axis=0, concat_axis=1, tiled=True)[0]
    output = gating * (convolved + skip_gain[None, :] * signal)
    return output.astype(jnp.bfloat16)


LANES = 128
FILTER, SIGNAL, BACK, SHELF, ACROSS = range(5)


def wave_tables(tokens):
    steps = (2 * np.arange(tokens)[:, None] + 1) * np.arange(tokens)[None, :] % (4 * tokens)
    angles = steps.astype(np.float64) * (math.pi / (2 * tokens))
    table = np.concatenate([np.cos(angles), np.sin(angles)], axis=0)
    bf16 = jnp.bfloat16
    high = table.astype(np.float32).astype(bf16)
    low = (table - high.astype(np.float64)).astype(np.float32).astype(bf16)
    return high, low, np.ascontiguousarray(high.T)


def fused_kernel(
    n, pdev, x_hbm, lib_hbm, slot_hbm, pref_hbm, taps_hbm, filt_hbm, skip_hbm, fhi_hbm, flo_hbm, g_hbm,
    out_ref,
    x_ref, lib_ref, slot_ref, pref_ref, taps_ref, filt_ref, skip_ref, fhi, flo, gmat, hsend, hrecv, ssend, srecv, ysend, yrecv, libsend, libg, lastsend, lastg,
    halosend, halorecv, ext, gate, cach, hspec, prod, rising,
    load_sem, send_sem, recv_sem, halo_send, halo_recv, last_send, last_recv,
):
    f32, bf16 = jnp.float32, jnp.bfloat16
    rows = x_ref.shape[1]
    tokens = rows * n
    prefix = pdev * rows
    duo = rows // 2
    steps = tokens // 2
    phases = range(2)
    wide = [slice(p * LANES, (p + 1) * LANES) for p in phases]
    me = lax.axis_index("seq")
    group = lax.axis_index("group")
    share = rows // 4
    barrier = pltpu.get_barrier_semaphore()
    for d in range(1, n):
        pl.semaphore_signal(
            barrier, inc=1, device_id={"seq": lax.rem(me + d, n)}, device_id_type=pl.DeviceIdType.MESH
        )
    pl.semaphore_signal(
        barrier, inc=1, device_id={"group": 1 - group}, device_id_type=pl.DeviceIdType.MESH
    )
    operands = [
        *((filt_hbm.at[:, j * LANES : (j + 1) * LANES], filt_ref.at[j]) for j in range(n)), (x_hbm, x_ref), (lib_hbm, lib_ref), (taps_hbm, taps_ref),
        (slot_hbm, slot_ref), (pref_hbm, pref_ref), (skip_hbm, skip_ref),
        (fhi_hbm, fhi), (flo_hbm, flo), (g_hbm, gmat),
    ]
    loads = [pltpu.make_async_copy(src, dst, load_sem.at[i]) for i, (src, dst) in enumerate(operands)]
    for load in loads:
        load.start()
    load_filter, load_x, load_small, load_tables = loads[:n], loads[n], loads[n + 1 : -3], loads[-3:]

    half_ring = n // 2
    order = [d for k in range(1, half_ring) for d in (k, n - k)] + [half_ring]

    def lanes_of(index):
        if isinstance(index, int):
            return pl.ds(index * LANES, LANES)
        return pl.ds(pl.multiple_of(index * LANES, LANES), LANES)

    def remote(src, dst, send, recv, peer):
        return pltpu.make_async_remote_copy(
            src_ref=src, dst_ref=dst, send_sem=send, recv_sem=recv,
            device_id={"seq": peer}, device_id_type=pl.DeviceIdType.MESH,
        )

    def at_rows(ref, index):
        return ref.at[pl.ds(pl.multiple_of(index * duo, duo), duo)]

    def at_share(ref, index):
        return ref.at[pl.ds(pl.multiple_of(index * duo + group * share, share), share)]

    def across(d):
        part = at_share(hrecv, lax.rem(me + n - d, n))
        return pltpu.make_async_remote_copy(
            src_ref=part, dst_ref=part, send_sem=send_sem.at[ACROSS, d], recv_sem=recv_sem.at[ACROSS, d],
            device_id={"group": 1 - group}, device_id_type=pl.DeviceIdType.MESH,
        )

    def move(kind, d):
        peer = lax.rem(me + d, n)
        source, target = {
            FILTER: (
                hsend.at[peer, pl.ds(pl.multiple_of(group * share, share), share)],
                at_share(hrecv, me),
            ),
            SIGNAL: (ssend.at[peer], at_rows(srecv, me)),
            BACK: (ysend.at[peer], yrecv.at[me]),
            SHELF: (libsend.at[peer], libg.at[me]),
        }[kind]
        return remote(source, target, send_sem.at[kind, d], recv_sem.at[kind, d], peer)

    def arrived(kind):
        for d in range(1, n):
            move(kind, d).wait_recv()

    halo_copy = remote(halosend, halorecv, halo_send, halo_recv, lax.rem(me + 1, n))
    others = [s for s in range(n) if s != pdev]
    last_copy = {
        s: remote(lastsend, lastg.at[me], last_send, last_recv.at[s], pdev) for s in others
    }

    def strided(start, count):
        return pl.ds(start, count, stride=2)

    for j in range(n):
        load_filter[j].wait()
        for p in phases:
            hsend[j, :, wide[p]] = filt_ref[j, strided(p, duo), :].astype(bf16)
    at_rows(hrecv, me)[...] = hsend[me]
    load_x.wait()
    for j in range(3):
        for c in range(n):
            ext[j, c, 8:] = x_ref[j, :, c * LANES : (c + 1) * LANES].astype(f32)
        halosend[2 * j : 2 * j + 2] = x_ref[j, rows - 16 :].astype(f32)[14:]
    halosend[6:] = jnp.zeros((2, halosend.shape[1]), f32)
    for load in load_small:
        load.wait()
    shelf = lib_ref[0].astype(f32)
    for j in range(n):
        cols = slice(j * LANES, (j + 1) * LANES)
        libsend[j] = shelf[:, cols]
        lastsend[2 * j : 2 * j + 2] = shelf[6:, cols]
    libg[me] = libsend[me]
    lastg[me] = lastsend[...]

    pl.semaphore_wait(barrier, n)

    @pl.when(me < n - 1)
    def _():
        halo_copy.start()

    for s in others:
        @pl.when(me == s)
        def _():
            last_copy[s].start()

    for d in order:
        move(FILTER, d).start()
    for d in order:
        move(SHELF, d).start()
    @pl.when(me == 0)
    def _():
        halorecv[...] = jnp.zeros_like(halorecv)

    @pl.when(me > 0)
    def _():
        halo_copy.wait_recv()

    for j in range(3):
        for c in range(n):
            ext[j, c, 6:8] = halorecv[2 * j : 2 * j + 2, c * LANES : (c + 1) * LANES]

    per_row = pref_ref.shape[0]

    def wanted(b):
        return slot_ref[pref_ref[b % per_row, b // per_row]]

    blocks = prefix // BLK

    @pl.when(me == pdev)
    def _():
        for s in others:
            last_copy[s].wait_recv()
        ends = lastg[wanted(blocks - 1)]
        for j in range(n):
            ext[2, j, 6:8] = ends[2 * j : 2 * j + 2]

    def short(j, p, index):
        cols = lanes_of(index)
        return (
            taps_ref[0, j : j + 1, cols] * ext[j, index, strided(8 + p, duo), :]
            + taps_ref[1, j : j + 1, cols] * ext[j, index, strided(7 + p, duo), :]
            + taps_ref[2, j : j + 1, cols] * ext[j, index, strided(6 + p, duo), :]
        )

    in_prefix = me < pdev

    def pack_signal(index):
        for p in phases:
            factor = jnp.where(in_prefix, jnp.float32(1.0), short(2, p, index))
            ssend[index, :, wide[p]] = (short(1, p, index) * factor).astype(bf16)

    for d in order:
        pack_signal(lax.rem(me + d, n))
        move(SIGNAL, d).start()
    pack_signal(me)
    at_rows(srecv, me)[...] = ssend[me]
    for d in range(1, n):
        move(FILTER, d).wait_recv()
        across(d).start()

    own = lanes_of(me)
    arrived(SHELF)
    cach[:8] = jnp.zeros((8, LANES), f32)
    for b in range(blocks):
        cach[8 + BLK * b : 8 + BLK * (b + 1)] = libg[wanted(b)]

    for d in range(1, n):
        across(d).wait_recv()
    for load in load_tables:
        load.wait()
    tile = 256
    skip = skip_ref[own].reshape(1, LANES)

    def filter_tile(i, carry):
        span = pl.ds(pl.multiple_of(i * tile, tile), tile)
        spec = jnp.dot(fhi[span], hrecv[...], preferred_element_type=f32)
        spec += jnp.dot(flo[span], hrecv[...], preferred_element_type=f32)
        hspec[span, wide[0]] = spec[:, wide[0]] + jnp.where(i < steps // tile, skip, 0.0)
        hspec[span, wide[1]] = spec[:, wide[1]]
        return carry

    lax.fori_loop(0, 2 * steps // tile, filter_tile, 0)

    for j in range(n):
        for p in phases:
            gate[j, :, wide[p]] = short(0, p, j)

    early = prefix // 2
    cached = [
        taps_ref[0, 2:3, own] * cach[strided(8 + p, early), :]
        + taps_ref[1, 2:3, own] * cach[strided(7 + p, early), :]
        + taps_ref[2, 2:3, own] * cach[strided(6 + p, early), :]
        for p in phases
    ]
    arrived(SIGNAL)
    for p in phases:
        srecv[:early, wide[p]] = (srecv[:early, wide[p]].astype(f32) * cached[p]).astype(bf16)

    half = 128

    def times(first, second):
        return (
            first[0] * second[0] - first[1] * second[1],
            first[0] * second[1] + first[1] * second[0],
        )

    def signal_tile(i, carry):
        spans = [pl.ds(pl.multiple_of(part * steps + i * half, half), half) for part in range(2)]
        waves = [
            jnp.dot(fhi[span], srecv[...], preferred_element_type=f32)
            + jnp.dot(flo[span], srecv[...], preferred_element_type=f32)
            for span in spans
        ]
        taps = [hspec[span] * (1.0 / steps) for span in spans]
        turn = [fhi[span, 1:2].astype(f32) + flo[span, 1:2].astype(f32) for span in spans]
        even, odd = ([wave[:, wide[p]] for wave in waves] for p in phases)
        tap_even, tap_odd = ([tap[:, wide[p]] for tap in taps] for p in phases)
        late = times(times(odd, tap_odd), turn)
        even_even, even_odd, odd_even = times(even, tap_even), times(even, tap_odd), times(odd, tap_even)
        for part in range(2):
            for p, value in ((0, even_even[part] + late[part]), (1, even_odd[part] + odd_even[part])):
                high = value.astype(bf16)
                prod[spans[part], wide[p]] = high
                prod[spans[part], (2 + p) * LANES : (3 + p) * LANES] = (
                    value - high.astype(f32)
                ).astype(bf16)
        return carry

    lax.fori_loop(0, steps // half, signal_tile, 0)

    reach = half_ring * duo
    for k in (1, 0):
        side = lax.rem(me // half_ring + k, 2)
        span = pl.ds(pl.multiple_of(side * reach, reach), reach)
        both = jnp.dot(gmat[span], prod[...], preferred_element_type=f32)
        value = (both[:, : 2 * LANES] + both[:, 2 * LANES :]).astype(bf16)
        for r in range(half_ring):
            target = side * half_ring + r
            ysend[target] = value[r * duo : (r + 1) * duo]

            @pl.when(target != me)
            def _():
                move(BACK, lax.rem(target - me + n, n)).start()

    def finish(source, value):
        cols = lanes_of(source)
        for p in phases:
            rising[strided(p, duo), :] = gate[source, :, wide[p]] * value[:, wide[p]].astype(f32)
        out_ref[:, cols] = rising[...].astype(bf16)

    finish(me, ysend[me])
    for d in range(1, n):
        move(BACK, d).wait_recv()
        source = lax.rem(me + n - d, n)
        finish(source, yrecv[source])

    @pl.when(me < n - 1)
    def _():
        halo_copy.wait_send()

    @pl.when(me != pdev)
    def _():
        last_copy[others[0]].wait_send()

    for kind in (SHELF, FILTER, SIGNAL, BACK):
        for d in range(1, n):
            move(kind, d).wait_send()
    for d in range(1, n):
        across(d).wait_send()


def fused_body(n, fresh, library, block_slot, prefix_blocks, short_taps, long_filter, skip_gain):
    rows, channels = fresh.shape[0], fresh.shape[2]
    tokens = rows * n
    prefix = prefix_blocks.size * BLK
    f32, bf16 = jnp.float32, jnp.bfloat16
    high, low, turned = wave_tables(tokens // 2)
    far = pl.BlockSpec(memory_space=pltpu.HBM)
    dma = pltpu.SemaphoreType.DMA
    return pl.pallas_call(
        functools.partial(fused_kernel, n, prefix // rows),
        out_shape=jax.ShapeDtypeStruct((rows, channels), bf16),
        in_specs=[far] * 10,
        out_specs=pl.BlockSpec(memory_space=pltpu.VMEM),
        scratch_shapes=[
            pltpu.VMEM((3, rows, channels), bf16),
            pltpu.VMEM(library.shape, bf16),
            pltpu.SMEM(block_slot.shape, jnp.int32),
            pltpu.SMEM(prefix_blocks.shape[::-1], jnp.int32),
            pltpu.VMEM(short_taps.shape, f32),
            pltpu.VMEM((n, rows, LANES), f32),
            pltpu.VMEM(skip_gain.shape, f32),
            pltpu.VMEM((tokens, tokens // 2), bf16),
            pltpu.VMEM((tokens, tokens // 2), bf16),
            pltpu.VMEM((tokens // 2, tokens), bf16),
            pltpu.VMEM((n, rows // 2, 2 * LANES), bf16),
            pltpu.VMEM((tokens // 2, 2 * LANES), bf16),
            pltpu.VMEM((n, rows // 2, 2 * LANES), bf16),
            pltpu.VMEM((tokens // 2, 2 * LANES), bf16),
            pltpu.VMEM((n, rows // 2, 2 * LANES), bf16),
            pltpu.VMEM((n, rows // 2, 2 * LANES), bf16),
            pltpu.VMEM((n, BLK, LANES), f32),
            pltpu.VMEM((n, BLK, LANES), f32),
            pltpu.VMEM((2 * n, LANES), f32),
            pltpu.VMEM((n, 2 * n, LANES), f32),
            pltpu.VMEM((8, channels), f32),
            pltpu.VMEM((8, channels), f32),
            pltpu.VMEM((3, n, rows + 8, LANES), f32),
            pltpu.VMEM((n, rows // 2, 2 * LANES), f32),
            pltpu.VMEM((prefix + 8, LANES), f32),
            pltpu.VMEM((tokens, 2 * LANES), f32),
            pltpu.VMEM((tokens, 4 * LANES), bf16),
            pltpu.VMEM((rows, LANES), f32),
            dma((9 + n,)),
            dma((5, n)),
            dma((5, n)),
            dma(()),
            dma(()),
            dma(()),
            dma((n,)),
        ],
        compiler_params=pltpu.CompilerParams(
            collective_id=0, has_side_effects=True, vmem_limit_bytes=63 * 1024 * 1024
        ),
    )(
        jnp.transpose(fresh, (1, 0, 2)), library, block_slot, prefix_blocks.T, short_taps, long_filter,
        skip_gain, jnp.asarray(high), jnp.asarray(low), jnp.asarray(turned),
    )


def body(groups, n, fresh, library, block_slot, prefix_blocks, short_taps, long_filter, skip_gain):
    rows, channels = fresh.shape[0], fresh.shape[2]
    prefix = prefix_blocks.size * BLK
    small = (
        groups == 2
        and rows * n <= 1024
        and rows % 128 == 0
        and channels == n * LANES
        and library.shape[0] == 1
        and prefix % rows == 0
        and 0 < prefix // rows <= n // 2
        and n % 2 == 0
    )
    chosen = functools.partial(fused_body, n) if small else long_body
    return chosen(fresh, library, block_slot, prefix_blocks, short_taps, long_filter, skip_gain)


def solution(mesh):
    return jax.shard_map(
        functools.partial(body, mesh.shape["group"], mesh.shape["seq"]),
        mesh=mesh,
        in_specs=(
            P(("group", "seq"), None, "chan"),
            P("seq", None, "chan"),
            P(),
            P("group", None),
            P(None, None, "chan"),
            P("seq", "chan"),
            P("chan"),
        ),
        out_specs=P(("group", "seq"), "chan"),
        check_vma=False,
    )
```
